32 devices in a mesh: seq: 16 (over z, x, core), fsdp: 2 (over y).
Axes of the slice: x: 2, y: 2, z: 4, core: 2. Of those that a mesh axis runs over, the one named last changes fastest.
Arguments:
- tokens: bfloat16 [2, 2048, 640], P('fsdp', 'seq'), may hold values from -30 to 30, as said below
- w_q: bfloat16 [640, 1024], P(None, 'fsdp'), may hold values from -0.25 to 0.25
- w_k: bfloat16 [640, 256], P(None, 'fsdp'), may hold values from -0.25 to 0.25
- w_v: bfloat16 [640, 256], P(None, 'fsdp'), may hold values from -0.25 to 0.25
- w_o: bfloat16 [1024, 640], P('fsdp'), may hold values from -0.1875 to 0.1875
- w_gate: bfloat16 [640, 2048], P(None, 'fsdp'), may hold values from -0.25 to 0.25
- w_up: bfloat16 [640, 2048], P(None, 'fsdp'), may hold values from -0.25 to 0.25
- w_down: bfloat16 [2048, 640], P('fsdp'), may hold values from -0.125 to 0.125
- gains: float32 [3072], replicated, may hold values from 0.25 to 1.75
- positions: int32 [2, 2048], P('fsdp', 'seq'), may hold values from 0 to 2173, as said below
- cotangent: bfloat16 [2, 2048, 640], P('fsdp', 'seq'), may hold values from -6 to 6
Outputs:
- outputs: bfloat16 [2, 2048, 640], P('fsdp', 'seq')
- d_tokens: float32 [2, 2048, 640], P('fsdp', 'seq')
- d_w_q: float32 [655360], P(('seq', 'fsdp'))
- d_w_k: float32 [163840], P(('seq', 'fsdp'))
- d_w_v: float32 [163840], P(('seq', 'fsdp'))
- d_w_o: float32 [655360], P(('seq', 'fsdp'))
- d_w_gate: float32 [1310720], P(('seq', 'fsdp'))
- d_w_up: float32 [1310720], P(('seq', 'fsdp'))
- d_w_down: float32 [1310720], P(('seq', 'fsdp'))
- d_gains: float32 [3072], P(('seq', 'fsdp'))
The draws below stay inside these ranges and needn't reach their ends.
Inputs may be any that keep to these rules, and one draw needn't show every extreme that they name: `tokens`: activations of order one with row scales that differ. Each sequence holds three documents end to end, positions counting from 0 at a document's start: the first continues an earlier text from a drawn offset and ends within the first 128 tokens, the second ends within the last 128 tokens, the third runs to the sequence's end.
All inputs are finite; a program needn't handle non-finite values.
Results may differ from the reference program's by a relative error of at most 0.017.
Values may be sent and summed in bfloat16 or wider, within the bound.
A program may use at most 128 MiB of HBM per device.

```python
import jax
import jax.numpy as jnp
from jax import lax

D = 640
HEADS = 4
HD = 256
FF = 2048
WINDOW = 512
TOK_DEV = 128
SEQ_LEN = 2048
SEQS = 2
QW = 1024
GAINS = 3072


def draw_tokens(key, part):
    key = jax.random.fold_in(key, 5)
    base_key, row_key, col_key = jax.random.split(key, 3)
    base = jax.random.normal(base_key, (SEQS, SEQ_LEN, D), jnp.float32)
    row_scale = jnp.exp(jax.random.uniform(row_key, (SEQS, SEQ_LEN, 1), jnp.float32, -1.15, 1.15))
    col_scale = jnp.exp(jax.random.uniform(col_key, (1, 1, D), jnp.float32, -0.35, 0.35))
    return jnp.clip(base * row_scale * col_scale, -30.0, 30.0).astype(jnp.bfloat16)


def draw_positions(key, part):
    key = jax.random.fold_in(key, 11)
    offset_key, first_key, last_key = jax.random.split(key, 3)
    offset = jax.random.randint(offset_key, (SEQS, 1), 0, SEQ_LEN)
    first_end = jax.random.randint(first_key, (SEQS, 1), 1, TOK_DEV)
    last_start = jax.random.randint(last_key, (SEQS, 1), SEQ_LEN - TOK_DEV + 1, SEQ_LEN)
    index = jnp.arange(SEQ_LEN, dtype=jnp.int32)[None, :]
    middle = jnp.where(index < last_start, index - first_end, index - last_start)
    return jnp.where(index < first_end, offset + index, middle).astype(jnp.int32)


def level_of(key, extent, pieces, low, top_value):
    gain, own = 1.0, jax.random.fold_in(key, 6)
    for dim, parts in pieces:
        steps = jnp.exp(jax.random.uniform(jax.random.fold_in(own, dim), (parts,), jnp.float32, low / len(pieces), top_value / len(pieces)))
        gain = gain * jnp.repeat(steps, extent[dim] // parts).reshape([-1 if axis == dim else 1 for axis in range(len(extent))])
    return gain


def noise(rng, dims, spread, limit, cuts=(), kind=jnp.bfloat16):
    result = spread * jax.random.normal(rng, dims, jnp.float32)
    if cuts:
        result = result * level_of(rng, dims, cuts, -0.22, 0.18)
    return jnp.clip(result, -limit, limit).astype(kind)


def setup_inputs(seed: int = 0) -> dict:
    arg_keys = jax.random.split(jax.random.key(seed), 12)
    tokens = draw_tokens(jax.random.fold_in(arg_keys[11], 71), 0)
    w_q = noise(arg_keys[1], (D, QW), D ** -0.5, 0.25, ((1, 2),))
    w_k = noise(arg_keys[2], (D, HD), D ** -0.5, 0.25, ((1, 2),))
    w_v = noise(arg_keys[3], (D, HD), D ** -0.5, 0.25, ((1, 2),))
    w_o = noise(arg_keys[4], (QW, D), QW ** -0.5, 0.1875, ((0, 2),))
    w_gate = noise(arg_keys[5], (D, FF), D ** -0.5, 0.25, ((1, 2),))
    w_up = noise(arg_keys[6], (D, FF), D ** -0.5, 0.25, ((1, 2),))
    w_down = noise(arg_keys[7], (FF, D), FF ** -0.5, 0.125, ((0, 2),))
    gains = jnp.clip(1.0 + 0.15 * jax.random.normal(arg_keys[8], (GAINS,), jnp.float32), 0.25, 1.75)
    positions = draw_positions(jax.random.fold_in(arg_keys[11], 71), 0)
    cotangent = noise(arg_keys[10], (SEQS, SEQ_LEN, D), 1.0, 6.0, ((0, 2), (1, 16)))
    return {"tokens": tokens, "w_q": w_q, "w_k": w_k, "w_v": w_v, "w_o": w_o, "w_gate": w_gate, "w_up": w_up, "w_down": w_down, "gains": gains, "positions": positions, "cotangent": cotangent}


EPSILON = 1e-06
NEGATIVE = -1e+30
PRECISE = lax.Precision.HIGHEST

@jax.custom_vjp
def low(v):
    return lax.optimization_barrier(v.astype(jnp.bfloat16)).astype(jnp.float32)

@jax.custom_vjp
def low_back(v):
    return v

def low_keep(v):
    return (low(v), None)

def low_pass(kept, grad):
    return (grad,)

def back_keep(v):
    return (v, None)

def back_low(kept, grad):
    return (low(grad),)
low.defvjp(low_keep, low_pass)
low_back.defvjp(back_keep, back_low)

def rms_norm(vector, gain_vec):
    return vector * lax.rsqrt(lax.optimization_barrier(jnp.mean(vector * vector, axis=-1, keepdims=True)) + EPSILON) * gain_vec

def rotate(vector, places):
    half_size = vector.shape[-1] // 2
    inverse = 10000.0 ** (-2.0 * jnp.arange(half_size, dtype=jnp.float32) / vector.shape[-1])
    angles = places.astype(jnp.float32)[:, None] * inverse[None, :]
    cosine = jnp.cos(angles)
    sine_part = jnp.sin(angles)
    if vector.ndim == 3:
        cosine = cosine[:, None, :]
        sine_part = sine_part[:, None, :]
    first_half = vector[..., :half_size]
    second = vector[..., half_size:]
    return jnp.concatenate([first_half * cosine - second * sine_part, second * cosine + first_half * sine_part], axis=-1)

def attend(queries, keys_all, values_all, places):
    padding = jnp.zeros((WINDOW, HD), jnp.float32)
    keys_pad = jnp.concatenate([padding, keys_all], axis=0)
    values_pad = jnp.concatenate([padding, values_all], axis=0)
    row_ids = jnp.arange(WINDOW, dtype=jnp.int32)[:, None]
    col_ids = jnp.arange(2 * WINDOW, dtype=jnp.int32)[None, :]

    def one_block(number):
        start_row = number * WINDOW
        query_rows = lax.dynamic_slice_in_dim(queries, start_row, WINDOW, 0)
        key_rows = lax.dynamic_slice_in_dim(keys_pad, start_row, 2 * WINDOW, 0)
        value_rows = lax.dynamic_slice_in_dim(values_pad, start_row, 2 * WINDOW, 0)
        place_rows = lax.dynamic_slice_in_dim(places, start_row, WINDOW, 0)
        raw_scores = jnp.einsum('thd,jd->htj', query_rows, key_rows, precision=PRECISE) * HD ** (-0.5)
        distance = row_ids - col_ids + WINDOW
        allowed = (distance >= 0) & (distance <= jnp.minimum(place_rows[:, None], WINDOW - 1)) & (start_row - WINDOW + col_ids >= 0)
        scores = low_back(jnp.where(allowed[None], raw_scores, NEGATIVE))
        exponent = jnp.exp(scores - lax.optimization_barrier(jnp.max(scores, axis=-1, keepdims=True)))
        probs = low(exponent / lax.optimization_barrier(jnp.sum(exponent, axis=-1, keepdims=True)))
        return jnp.einsum('htj,jd->thd', probs, value_rows, precision=PRECISE)
    blocks = lax.map(jax.checkpoint(one_block), jnp.arange(SEQ_LEN // WINDOW, dtype=jnp.int32))
    return blocks.reshape(SEQ_LEN, HEADS * HD)

def layer(tokens_f, w_q, w_k, w_v, w_o, w_gate, w_up, w_down, gains, places):
    gain_in = gains[0:D]
    gain_attn = gains[D:2 * D]
    gain_mlp = gains[2 * D:3 * D]
    gain_out = gains[3 * D:4 * D]
    gain_query = gains[4 * D:4 * D + HD]
    gain_key = gains[4 * D + HD:4 * D + 2 * HD]
    normed = low(rms_norm(tokens_f, gain_in))
    q_raw = low_back(jnp.dot(normed, w_q, precision=PRECISE))
    k_raw = low_back(jnp.dot(normed, w_k, precision=PRECISE))
    v_raw = low(low_back(jnp.dot(normed, w_v, precision=PRECISE)))
    queries = low(rotate(rms_norm(q_raw.reshape(SEQ_LEN, HEADS, HD), gain_query), places))
    keys_all = low(rotate(rms_norm(k_raw, gain_key), places))
    attended = low(low_back(attend(queries, keys_all, v_raw, places)))
    attn_raw = low_back(jnp.dot(attended, w_o, precision=PRECISE))
    residual = tokens_f + rms_norm(attn_raw, gain_attn)
    ffn_in = low(rms_norm(residual, gain_mlp))
    gate_raw = low_back(jnp.dot(ffn_in, w_gate, precision=PRECISE))
    up_raw = low_back(jnp.dot(ffn_in, w_up, precision=PRECISE))
    hidden = low(jax.nn.gelu(gate_raw, approximate=True) * up_raw)
    down_raw = low_back(jnp.dot(hidden, w_down, precision=PRECISE))
    return residual + rms_norm(down_raw, gain_out)

def reference(tokens, w_q, w_k, w_v, w_o, w_gate, w_up, w_down, gains, positions, cotangent):
    weights = (w_q.astype(jnp.float32), w_k.astype(jnp.float32), w_v.astype(jnp.float32), w_o.astype(jnp.float32), w_gate.astype(jnp.float32), w_up.astype(jnp.float32), w_down.astype(jnp.float32), gains)

    def per_sequence(running, sequence):
        seq_tokens, seq_cot, seq_places = sequence

        def forward(tokens_f, *params):
            return layer(tokens_f, *params, seq_places)
        output, pullback = jax.vjp(forward, seq_tokens.astype(jnp.float32), *weights)
        gradients = pullback(seq_cot.astype(jnp.float32))
        summed = jax.tree.map(lambda before, increment: before + increment, running, tuple(gradients[1:]))
        return (summed, (output.astype(jnp.bfloat16), gradients[0]))
    start_sums = jax.tree.map(jnp.zeros_like, weights)
    totals, (outputs, d_tokens) = lax.scan(per_sequence, start_sums, (tokens, cotangent, positions))
    return (outputs, d_tokens, totals[0].reshape(-1), totals[1].reshape(-1), totals[2].reshape(-1), totals[3].reshape(-1), totals[4].reshape(-1), totals[5].reshape(-1), totals[6].reshape(-1), totals[7])
```

```python
import jax
import jax.numpy as jnp
from jax import lax
from jax.sharding import PartitionSpec as P

D = 640
HEADS = 4
HD = 256
WINDOW = 512
TOK_DEV = 128


EPSILON = 1e-06
NEGATIVE = -1e30


def shifted(value, axis, steps):
    count = lax.axis_size(axis)
    leading, last = (max(0, -steps), min(count, count - steps))
    return lax.ppermute(value, axis, [(source, source + steps) for source in range(leading, last)])


def rms_norm(vector, gain_vec):
    return (
        vector * lax.rsqrt(jnp.mean(vector * vector, axis=-1, keepdims=True) + EPSILON) * gain_vec
    )


def rotate(vector, places):
    half_size = vector.shape[-1] // 2
    inverse = 10000.0 ** (-2.0 * jnp.arange(half_size, dtype=jnp.float32) / vector.shape[-1])
    angles = places.astype(jnp.float32)[:, None] * inverse[None, :]
    cosine = jnp.cos(angles)
    sine_part = jnp.sin(angles)
    if vector.ndim == 3:
        cosine = cosine[:, None, :]
        sine_part = sine_part[:, None, :]
    first_half = vector[..., :half_size]
    second = vector[..., half_size:]
    return jnp.concatenate(
        [first_half * cosine - second * sine_part, second * cosine + first_half * sine_part],
        axis=-1,
    )


def queries_keys(q_raw, k_raw, gain_query, gain_key, places):
    queries = rotate(rms_norm(q_raw.reshape(q_raw.shape[0], q_raw.shape[1] // HD, HD), gain_query), places)
    return (queries, rotate(rms_norm(k_raw, gain_key), places))


def gelu_mix(gate_raw, up_raw):
    return jax.nn.gelu(gate_raw, approximate=True) * up_raw


def matmul(left_side, right_side):
    return jnp.dot(left_side, right_side, preferred_element_type=jnp.float32)


def inner_left(left_side, right_side):
    return lax.dot_general(
        left_side, right_side, (((0,), (0,)), ((), ())), preferred_element_type=jnp.float32
    )


def inner_right(left_side, right_side):
    return lax.dot_general(
        left_side, right_side, (((1,), (1,)), ((), ())), preferred_element_type=jnp.float32
    )


def swapped(value):
    return lax.ppermute(value, "fsdp", [(0, 1), (1, 0)])


def pair_sum(partial):
    half = partial.shape[0] // 2
    far = swapped(partial.astype(jnp.bfloat16)).astype(jnp.float32)
    return partial + jnp.concatenate([far[half:], far[:half]], axis=0)


def flat_rows(piece, fsdp):
    other = swapped(piece)
    whole = jnp.where(
        fsdp == 0,
        jnp.concatenate([piece, other], axis=1),
        jnp.concatenate([other, piece], axis=1),
    ).reshape(2, -1)
    return lax.dynamic_index_in_dim(whole, fsdp, 0, keepdims=False)


def reduce_generic(columns, rows, fsdp):
    count = lax.axis_size("seq")
    packed = jnp.concatenate(
        [value.astype(jnp.bfloat16).reshape(count, -1) for value in columns + rows], axis=1
    )
    mine = lax.psum_scatter(packed, "seq", scatter_dimension=0, tiled=True)
    mine = mine.astype(jnp.float32).reshape(-1)
    results = []
    start = 0
    for value in columns:
        size = value.size // count
        piece = mine[start : start + size].reshape(-1, value.shape[1])
        results.append(flat_rows(piece, fsdp))
        start += size
    moves = []
    for plane in range(2):
        for chunk in range(count):
            target = (count // 2) * plane + chunk // 2
            moves.append((chunk * 2 + plane, target * 2 + chunk % 2))
    for value in rows:
        size = value.size // count
        results.append(lax.ppermute(mine[start : start + size], ("seq", "fsdp"), moves))
        start += size
    return results


def per_device(tokens, w_q, w_k, w_v, w_o, w_gate, w_up, w_down, gains, positions, cotangent):
    fsdp = lax.axis_index("fsdp")
    block = tokens.shape[1]
    own_pack = jnp.concatenate([tokens[0], cotangent[0]], axis=0)
    far_pack = swapped(own_pack)
    w_kv = jnp.concatenate([w_k, w_v], axis=1)
    far_kv = swapped(w_kv)
    half = w_k.shape[1]

    def widened(near, far):
        return jnp.where(
            fsdp == 0,
            jnp.concatenate([near, far], axis=1),
            jnp.concatenate([far, near], axis=1),
        )

    full_k = widened(w_kv[:, :half], far_kv[:, :half])
    full_v = widened(w_kv[:, half:], far_kv[:, half:])
    far_places = swapped(positions)
    places2 = jnp.concatenate([positions, far_places], axis=0)
    places = places2.reshape(-1)
    tokens_f = jnp.concatenate([tokens[0], far_pack[:block]], axis=0).astype(jnp.float32)
    d_out = jnp.concatenate([cotangent[0], far_pack[block:]], axis=0).astype(jnp.float32)
    gain_in = gains[0:D]
    gain_attn = gains[D : 2 * D]
    gain_mlp = gains[2 * D : 3 * D]
    gain_out = gains[3 * D : 4 * D]
    gain_query = gains[4 * D : 4 * D + HD]
    gain_key = gains[4 * D + HD : 4 * D + 2 * HD]
    normed = rms_norm(tokens_f, gain_in)
    normed_b = normed.astype(jnp.bfloat16)
    q_raw = matmul(normed_b, w_q)
    k_raw = matmul(normed_b, full_k)
    v_raw = matmul(normed_b, full_v)

    def rotary(q_part, k_part, gq_part, gk_part):
        return queries_keys(q_part, k_part, gq_part, gk_part, places)

    (queries, keys_own), pull_rot = jax.vjp(rotary, q_raw, k_raw, gain_query, gain_key)
    heads = queries.shape[1]
    queries_b = queries.astype(jnp.bfloat16).reshape(2, block, heads, HD)
    kv_b = jnp.concatenate([keys_own, v_raw], axis=1).astype(jnp.bfloat16)
    kv_b = kv_b.reshape(2, block, 2 * HD)
    reach = WINDOW // block
    parts = [shifted(kv_b, "seq", distance) for distance in range(reach, 0, -1)]
    kv_all = jnp.concatenate(parts + [kv_b], axis=1)
    keys_all = kv_all[:, :, :HD]
    values_all = kv_all[:, :, HD:]
    span = (reach + 1) * block
    row_ids = jnp.arange(block, dtype=jnp.int32)[:, None]
    col_ids = jnp.arange(span, dtype=jnp.int32)[None, :]
    offsets = row_ids - col_ids + reach * block
    first_key = (lax.axis_index("seq") - reach) * block
    allowed = (
        (offsets >= 0)[None]
        & (offsets[None] <= jnp.minimum(places2[:, :, None], WINDOW - 1))
        & (first_key + col_ids >= 0)[None]
    )
    factor = HD ** (-0.5)
    raw_scores = (
        jnp.einsum("bthd,bkd->bhtk", queries_b, keys_all, preferred_element_type=jnp.float32)
        * factor
    )
    scores = jnp.where(allowed[:, None], raw_scores, NEGATIVE)
    exponent = jnp.exp(scores - jnp.max(scores, axis=-1, keepdims=True))
    probs_f = exponent / jnp.sum(exponent, axis=-1, keepdims=True)
    probs_b = probs_f.astype(jnp.bfloat16)
    attended = jnp.einsum(
        "bhtk,bkd->bthd", probs_b, values_all, preferred_element_type=jnp.float32
    )
    attended_b = attended.reshape(2 * block, heads * HD).astype(jnp.bfloat16)
    attn_raw = pair_sum(matmul(attended_b, w_o))
    attn_normed, pull_attn = jax.vjp(rms_norm, attn_raw, gain_attn)
    residual = tokens_f + attn_normed
    ffn_in, pull_mlp = jax.vjp(rms_norm, residual, gain_mlp)
    ffn_b = ffn_in.astype(jnp.bfloat16)
    gate_raw = matmul(ffn_b, w_gate)
    up_raw = matmul(ffn_b, w_up)
    hidden, pull_mix = jax.vjp(gelu_mix, gate_raw, up_raw)
    hidden_b = hidden.astype(jnp.bfloat16)
    down_raw = pair_sum(matmul(hidden_b, w_down))
    down_normed, pull_out = jax.vjp(rms_norm, down_raw, gain_out)
    output_b = (residual[:block] + down_normed[:block]).astype(jnp.bfloat16)
    d_down, d_gain_out = pull_out(d_out)
    d_down_b = d_down.astype(jnp.bfloat16)
    grad_down = inner_left(hidden_b, d_down_b)
    d_hidden = inner_right(d_down_b, w_down)
    d_gate, d_up = pull_mix(d_hidden)
    d_gate_b = d_gate.astype(jnp.bfloat16)
    d_up_b = d_up.astype(jnp.bfloat16)
    d_ffn = pair_sum(inner_right(d_gate_b, w_gate) + inner_right(d_up_b, w_up))
    grad_gate = inner_left(ffn_b, d_gate_b)
    grad_up = inner_left(ffn_b, d_up_b)
    d_from_mlp, d_gain_mlp = pull_mlp(d_ffn)
    d_residual = d_out + d_from_mlp
    d_attn, d_gain_attn = pull_attn(d_residual)
    d_attn_b = d_attn.astype(jnp.bfloat16)
    grad_o = inner_left(attended_b, d_attn_b)
    d_attended = inner_right(d_attn_b, w_o).astype(jnp.bfloat16).reshape(2, block, heads, HD)
    d_probs = jnp.einsum(
        "bthd,bkd->bhtk", d_attended, values_all, preferred_element_type=jnp.float32
    )
    row_total = jnp.sum(probs_f * d_probs, axis=-1, keepdims=True)
    d_scores = (probs_f * (d_probs - row_total)).astype(jnp.bfloat16)
    d_keys = (
        jnp.einsum("bhtk,bthd->bkd", d_scores, queries_b, preferred_element_type=jnp.float32)
        * factor
    )
    d_values = jnp.einsum(
        "bhtk,bthd->bkd", probs_b, d_attended, preferred_element_type=jnp.float32
    )
    d_kv = jnp.concatenate([d_keys, d_values], axis=2)
    d_kv_far = d_kv[:, : reach * block].astype(jnp.bfloat16)
    d_kv_own = d_kv[:, reach * block :]
    for distance in range(1, reach + 1):
        lower = (reach - distance) * block
        d_kv_own = d_kv_own + shifted(
            d_kv_far[:, lower : lower + block], "seq", -distance
        ).astype(jnp.float32)
    d_kv_own = pair_sum(d_kv_own).reshape(2 * block, 2 * HD)
    d_queries = (
        jnp.einsum("bhtk,bkd->bthd", d_scores, keys_all, preferred_element_type=jnp.float32)
        * factor
    ).reshape(2 * block, heads, HD)
    d_q_raw, d_k_raw, d_gain_query, d_gain_key = pull_rot((d_queries, d_kv_own[:, :HD]))
    d_q_b = d_q_raw.astype(jnp.bfloat16)
    d_kv_b = jnp.concatenate([d_k_raw, d_kv_own[:, HD:]], axis=1).astype(jnp.bfloat16)
    from_q = inner_right(d_q_b, w_q)
    far_q = swapped(from_q[block:].astype(jnp.bfloat16)).astype(jnp.float32)
    grad_q = inner_left(normed_b, d_q_b)
    d_k_half = lax.dynamic_slice_in_dim(d_kv_b[:, :HD], fsdp * half, half, 1)
    d_v_half = lax.dynamic_slice_in_dim(d_kv_b[:, HD:], fsdp * half, half, 1)
    grad_k = inner_left(normed_b, d_k_half)
    grad_v = inner_left(normed_b, d_v_half)
    d_normed = (
        from_q[:block]
        + far_q
        + inner_right(d_kv_b[:block, :HD], full_k)
        + inner_right(d_kv_b[:block, HD:], full_v)
    )
    d_from_in, d_gain_in = jax.vjp(rms_norm, tokens_f[:block], gain_in)[1](d_normed)
    d_tokens = d_residual[:block] + d_from_in
    grad_gains = jnp.concatenate(
        [
            d_gain_in,
            0.5 * d_gain_attn,
            0.5 * d_gain_mlp,
            0.5 * d_gain_out,
            d_gain_query,
            0.5 * d_gain_key,
        ]
    )
    flat_gate, flat_up, flat_down = reduce_generic([grad_gate, grad_up], [grad_down], fsdp)
    flat_q, flat_k, flat_v, flat_o = reduce_generic([grad_q, grad_k, grad_v], [grad_o], fsdp)
    flat_gains = lax.psum_scatter(
        grad_gains, ("seq", "fsdp"), scatter_dimension=0, tiled=True
    )
    return (
        output_b[None],
        d_tokens[None],
        flat_q,
        flat_k,
        flat_v,
        flat_o,
        flat_gate,
        flat_up,
        flat_down,
        flat_gains,
    )


def solution(mesh):
    in_specs = (
        P("fsdp", "seq", None),
        P(None, "fsdp"),
        P(None, "fsdp"),
        P(None, "fsdp"),
        P("fsdp", None),
        P(None, "fsdp"),
        P(None, "fsdp"),
        P("fsdp", None),
        P(),
        P("fsdp", "seq"),
        P("fsdp", "seq", None),
    )
    out_specs = (
        P("fsdp", "seq", None),
        P("fsdp", "seq", None),
        P(("seq", "fsdp")),
        P(("seq", "fsdp")),
        P(("seq", "fsdp")),
        P(("seq", "fsdp")),
        P(("seq", "fsdp")),
        P(("seq", "fsdp")),
        P(("seq", "fsdp")),
        P(("seq", "fsdp")),
    )
    return jax.shard_map(
        per_device, mesh=mesh, in_specs=in_specs, out_specs=out_specs, check_vma=False
    )
```

```python
import jax
import jax.numpy as jnp
from jax import lax
from jax.experimental import pallas as pl
from jax.experimental.pallas import tpu as pltpu
from jax.sharding import PartitionSpec as P

D = 640
HEADS = 4
HD = 256
WINDOW = 512
TOK_DEV = 128


EPSILON = 1e-06
NEGATIVE = -1e30


def shifted(value, axis, steps):
    count = lax.axis_size(axis)
    leading, last = (max(0, -steps), min(count, count - steps))
    return lax.ppermute(value, axis, [(source, source + steps) for source in range(leading, last)])


def rms_norm(vector, gain_vec):
    return (
        vector * lax.rsqrt(jnp.mean(vector * vector, axis=-1, keepdims=True) + EPSILON) * gain_vec
    )


def rotate(vector, places):
    half_size = vector.shape[-1] // 2
    inverse = 10000.0 ** (-2.0 * jnp.arange(half_size, dtype=jnp.float32) / vector.shape[-1])
    angles = places.astype(jnp.float32)[:, None] * inverse[None, :]
    cosine = jnp.cos(angles)
    sine_part = jnp.sin(angles)
    if vector.ndim == 3:
        cosine = cosine[:, None, :]
        sine_part = sine_part[:, None, :]
    first_half = vector[..., :half_size]
    second = vector[..., half_size:]
    return jnp.concatenate(
        [first_half * cosine - second * sine_part, second * cosine + first_half * sine_part],
        axis=-1,
    )


def queries_keys(q_raw, k_raw, gain_query, gain_key, places):
    queries = rotate(rms_norm(q_raw.reshape(q_raw.shape[0], q_raw.shape[1] // HD, HD), gain_query), places)
    return (queries, rotate(rms_norm(k_raw, gain_key), places))


def gelu_mix(gate_raw, up_raw):
    return jax.nn.gelu(gate_raw, approximate=True) * up_raw


def matmul(left_side, right_side):
    return jnp.dot(left_side, right_side, preferred_element_type=jnp.float32)


def inner_left(left_side, right_side):
    return lax.dot_general(
        left_side, right_side, (((0,), (0,)), ((), ())), preferred_element_type=jnp.float32
    )


def inner_right(left_side, right_side):
    return lax.dot_general(
        left_side, right_side, (((1,), (1,)), ((), ())), preferred_element_type=jnp.float32
    )


def swapped(value):
    return lax.ppermute(value, "fsdp", [(0, 1), (1, 0)])


def pair_sum(partial):
    half = partial.shape[0] // 2
    far = swapped(partial.astype(jnp.bfloat16)).astype(jnp.float32)
    return partial + jnp.concatenate([far[half:], far[:half]], axis=0)


def flat_rows(piece, fsdp):
    other = swapped(piece)
    whole = jnp.where(
        fsdp == 0,
        jnp.concatenate([piece, other], axis=1),
        jnp.concatenate([other, piece], axis=1),
    ).reshape(2, -1)
    return lax.dynamic_index_in_dim(whole, fsdp, 0, keepdims=False)


def reduce_generic(columns, rows, fsdp):
    count = lax.axis_size("seq")
    packed = jnp.concatenate(
        [value.astype(jnp.bfloat16).reshape(count, -1) for value in columns + rows], axis=1
    )
    mine = lax.psum_scatter(packed, "seq", scatter_dimension=0, tiled=True)
    mine = mine.astype(jnp.float32).reshape(-1)
    results = []
    start = 0
    for value in columns:
        size = value.size // count
        piece = mine[start : start + size].reshape(-1, value.shape[1])
        results.append(flat_rows(piece, fsdp))
        start += size
    moves = []
    for plane in range(2):
        for chunk in range(count):
            target = (count // 2) * plane + chunk // 2
            moves.append((chunk * 2 + plane, target * 2 + chunk % 2))
    for value in rows:
        size = value.size // count
        results.append(lax.ppermute(mine[start : start + size], ("seq", "fsdp"), moves))
        start += size
    return results


TALL = 80
WIDE = 1408
DEEP = 96


def reduce_kernel(
    a_ref,
    b_ref,
    g_ref,
    out_a,
    out_b,
    out_g,
    near_a,
    near_b,
    sum_a,
    sum_b,
    side_a,
    side_b,
    line_a,
    line_b,
    far_a,
    far_b,
    stage_a,
    stage_b,
    last_a,
    last_b,
    gain_sent,
    gain_got,
    send_near,
    recv_near,
    send_side,
    recv_side,
    send_far,
    recv_far,
    send_last,
    recv_last,
    send_gain,
    recv_gain,
):
    s = lax.axis_index("seq")
    f = lax.axis_index("fsdp")
    core = lax.rem(s, 2)
    chip = s // 2
    x = lax.rem(chip, 2)
    z = chip // 2
    mesh_id = pl.DeviceIdType.MESH
    sibling = (chip * 2 + 1 - core, f)
    beside = ((z * 2 + 1 - x) * 2 + core, f)
    across = (s, 1 - f)
    diagonal = (chip * 2 + 1 - core, 1 - f)
    along = [((lax.rem(z + d, 4) * 2 + x) * 2 + core, f) for d in range(4)]
    targets = [(8 * f + chip, k) for k in range(2)]
    sources = [(2 * lax.rem(s, 8) + c, s // 8) for c in range(2)]

    def elsewhere(place):
        return jnp.logical_or(place[0] != s, place[1] != f)

    barrier = pltpu.get_barrier_semaphore()
    greeted = [sibling, beside, across, diagonal] + along[1:]
    for place in greeted:
        pl.semaphore_signal(barrier, inc=1, device_id=place, device_id_type=mesh_id)
    others = jnp.int32(len(greeted))
    for place in targets + sources:
        others = others + elsewhere(place).astype(jnp.int32)

        @pl.when(elsewhere(place))
        def _():
            pl.semaphore_signal(barrier, inc=1, device_id=place, device_id_type=mesh_id)

    pl.semaphore_wait(barrier, others)

    def remote(source, target, sent, got, place):
        return pltpu.make_async_remote_copy(
            src_ref=source,
            dst_ref=target,
            send_sem=sent,
            recv_sem=got,
            device_id=place,
            device_id_type=mesh_id,
        )

    def part_a(unit, half):
        return a_ref.at[unit, :, pl.ds(pl.multiple_of(half * WIDE, 128), WIDE)]

    lines = [lax.rem(z + d, 4) for d in (2, 1, 3, 0)]

    def gain_copy(step, slot, place):
        return remote(
            gain_sent.at[step], gain_got.at[slot], send_gain.at[slot], recv_gain.at[slot], place
        )

    gain_sent[0] = g_ref[...]
    gain_near = gain_copy(0, 0, sibling)
    gain_near.start()
    near = []
    for xh in (1 - x, x):
        for zh in lines:
            unit = zh * 2 + xh
            near.append(
                (
                    remote(
                        part_a(unit, 1 - core),
                        near_a.at[unit],
                        send_near.at[0, unit],
                        recv_near.at[0, unit],
                        sibling,
                    ),
                    remote(
                        b_ref.at[unit, 1 - core],
                        near_b.at[unit],
                        send_near.at[1, unit],
                        recv_near.at[1, unit],
                        sibling,
                    ),
                )
            )
            for copy in near[-1]:
                copy.start()
    gain_near.wait()
    gain_sent[1] = gain_sent[0] + gain_got[0]
    gain_side = gain_copy(1, 1, beside)
    gain_side.start()
    side = []
    for step in range(4):
        zh = lines[step]
        unit = zh * 2 + 1 - x
        for copy in near[step]:
            copy.wait_recv()
        sum_a[step] = (
            part_a(unit, core)[...].astype(jnp.float32) + near_a[unit].astype(jnp.float32)
        ).astype(jnp.bfloat16)
        sum_b[step] = (
            b_ref[unit, core].astype(jnp.float32) + near_b[unit].astype(jnp.float32)
        ).astype(jnp.bfloat16)
        side.append(
            (
                remote(
                    sum_a.at[step],
                    side_a.at[step],
                    send_side.at[0, step],
                    recv_side.at[0, step],
                    beside,
                ),
                remote(
                    sum_b.at[step],
                    side_b.at[step],
                    send_side.at[1, step],
                    recv_side.at[1, step],
                    beside,
                ),
            )
        )
        for copy in side[-1]:
            copy.start()
    gain_side.wait()
    gain_sent[2] = gain_sent[1] + gain_got[1]
    gain_line = [gain_copy(2, 1 + d, along[d]) for d in (1, 2, 3)]
    for copy in gain_line:
        copy.start()
    far = []
    for step in range(4):
        unit = lines[step] * 2 + x
        for copy in near[4 + step]:
            copy.wait_recv()
        for copy in side[step]:
            copy.wait_recv()
        total_a = (
            part_a(unit, core)[...].astype(jnp.float32)
            + near_a[unit].astype(jnp.float32)
            + side_a[step].astype(jnp.float32)
        )
        total_b = (
            b_ref[unit, core].astype(jnp.float32)
            + near_b[unit].astype(jnp.float32)
            + side_b[step].astype(jnp.float32)
        )
        if step < 3:
            distance = (2, 1, 3)[step]
            line_a[step] = total_a.astype(jnp.bfloat16)
            line_b[step] = total_b.astype(jnp.bfloat16)
            far.append(
                (
                    remote(
                        line_a.at[step],
                        far_a.at[step],
                        send_far.at[0, step],
                        recv_far.at[0, step],
                        along[distance],
                    ),
                    remote(
                        line_b.at[step],
                        far_b.at[step],
                        send_far.at[1, step],
                        recv_far.at[1, step],
                        along[distance],
                    ),
                )
            )
            for copy in far[-1]:
                copy.start()
    for copy in gain_line:
        copy.wait()
    gain_sent[3] = (gain_sent[2] + gain_got[2]) + (gain_got[3] + gain_got[4])
    gain_cross = gain_copy(3, 5, across)
    gain_cross.start()
    for pair in far:
        for copy in pair:
            copy.wait_recv()
    total_a = total_a + far_a[0].astype(jnp.float32)
    total_a = total_a + far_a[1].astype(jnp.float32) + far_a[2].astype(jnp.float32)
    for k in range(4):
        stage_a[k, 0:20, :] = total_a[20 * k : 20 * k + 20]
        stage_a[k, 20:24, :] = jnp.zeros((4, WIDE), jnp.float32)
    total_b = total_b + far_b[0].astype(jnp.float32)
    total_b = total_b + far_b[1].astype(jnp.float32) + far_b[2].astype(jnp.float32)
    for k in range(2):
        stage_b[k] = total_b[48 * k : 48 * k + 48]
    me = 2 * core + f
    last = []
    for step, place in enumerate((across, diagonal, sibling)):
        goal = 2 * lax.rem(place[0], 2) + place[1]
        copy = remote(
            stage_a.at[goal], last_a.at[me], send_last.at[0, step], recv_last.at[0, step], place
        )
        copy.start()
        last.append(copy)
    moves = [
        remote(
            stage_b.at[k], last_b.at[core], send_last.at[1, k], recv_last.at[1, core], targets[k]
        )
        for k in range(2)
    ]
    for k in range(2):
        pl.when(elsewhere(targets[k]))(moves[k].start)

        @pl.when(jnp.logical_not(elsewhere(targets[k])))
        def _():
            last_b[core] = stage_b[k]

    last_a[me] = stage_a[me]
    gain_cross.wait()
    out_g[...] = gain_sent[3] + gain_got[5]
    for copy in last:
        copy.wait_recv()
    out_a[...] = last_a[...]
    for c in range(2):
        arrival = remote(
            stage_b.at[0], last_b.at[c], send_last.at[1, 0], recv_last.at[1, c], sibling
        )
        pl.when(elsewhere(sources[c]))(arrival.wait_recv)
    out_b[...] = last_b[...]
    for pair in near + side + far:
        for copy in pair:
            copy.wait_send()
    for copy in last:
        copy.wait_send()
    for k in range(2):
        pl.when(elsewhere(targets[k]))(moves[k].wait_send)


def reduce_planes(columns, rows, grad_gains, fsdp):
    low = jnp.bfloat16
    a = jnp.concatenate([value.astype(low) for value in columns], axis=1)
    a = a.reshape(8, TALL, 2 * WIDE)
    b = jnp.concatenate(
        [value.astype(low).reshape(8, 2, 2, -1, D).transpose(0, 2, 1, 3, 4) for value in rows],
        axis=3,
    ).reshape(8, 2, DEEP, D)
    f32 = jnp.float32
    vmem = pl.BlockSpec(memory_space=pltpu.VMEM)
    dma = pltpu.SemaphoreType.DMA
    last_a, last_b, gain_sum = pl.pallas_call(
        reduce_kernel,
        out_shape=(
            jax.ShapeDtypeStruct((4, 24, WIDE), f32),
            jax.ShapeDtypeStruct((2, DEEP // 2, D), f32),
            jax.ShapeDtypeStruct((24, 128), f32),
        ),
        in_specs=[vmem] * 3,
        out_specs=(vmem,) * 3,
        scratch_shapes=[
            pltpu.VMEM((8, TALL, WIDE), low),
            pltpu.VMEM((8, DEEP, D), low),
            pltpu.VMEM((4, TALL, WIDE), low),
            pltpu.VMEM((4, DEEP, D), low),
            pltpu.VMEM((4, TALL, WIDE), low),
            pltpu.VMEM((4, DEEP, D), low),
            pltpu.VMEM((3, TALL, WIDE), low),
            pltpu.VMEM((3, DEEP, D), low),
            pltpu.VMEM((3, TALL, WIDE), low),
            pltpu.VMEM((3, DEEP, D), low),
            pltpu.VMEM((4, 24, WIDE), f32),
            pltpu.VMEM((2, DEEP // 2, D), f32),
            pltpu.VMEM((4, 24, WIDE), f32),
            pltpu.VMEM((2, DEEP // 2, D), f32),
            pltpu.VMEM((4, 24, 128), f32),
            pltpu.VMEM((6, 24, 128), f32),
            dma((2, 8)),
            dma((2, 8)),
            dma((2, 4)),
            dma((2, 4)),
            dma((2, 3)),
            dma((2, 3)),
            dma((2, 3)),
            dma((2, 3)),
            dma((6,)),
            dma((6,)),
        ],
        compiler_params=pltpu.CompilerParams(
            collective_id=0, has_side_effects=True, vmem_limit_bytes=40 * 1024 * 1024
        ),
    )(a, b, grad_gains.reshape(24, 128))
    piece = last_a[:, :20].reshape(2, 2, 20, WIDE)
    halves = [jnp.concatenate([piece[0, plane], piece[1, plane]], axis=1) for plane in range(2)]
    results = []
    start = 0
    for value in columns:
        stop = start + value.shape[1]
        results.append(
            jnp.concatenate([half[:, start:stop] for half in halves], axis=1).reshape(-1)
        )
        start = stop
    start = 0
    for value in rows:
        stop = start + value.shape[0] // 32
        results.append(last_b[:, start:stop].reshape(-1))
        start = stop
    place = lax.axis_index("seq") * 2 + fsdp
    size = grad_gains.shape[0] // 32
    results.append(lax.dynamic_slice_in_dim(gain_sum.reshape(-1), place * size, size))
    return results


def per_device(tokens, w_q, w_k, w_v, w_o, w_gate, w_up, w_down, gains, positions, cotangent):
    fsdp = lax.axis_index("fsdp")
    block = tokens.shape[1]
    own_pack = jnp.concatenate([tokens[0], cotangent[0]], axis=0)
    far_pack = swapped(own_pack)
    w_kv = jnp.concatenate([w_k, w_v], axis=1)
    far_kv = swapped(w_kv)
    half = w_k.shape[1]

    def widened(near, far):
        return jnp.where(
            fsdp == 0,
            jnp.concatenate([near, far], axis=1),
            jnp.concatenate([far, near], axis=1),
        )

    full_k = widened(w_kv[:, :half], far_kv[:, :half])
    full_v = widened(w_kv[:, half:], far_kv[:, half:])
    far_places = swapped(positions)
    places2 = jnp.concatenate([positions, far_places], axis=0)
    places = places2.reshape(-1)
    tokens_f = jnp.concatenate([tokens[0], far_pack[:block]], axis=0).astype(jnp.float32)
    d_out = jnp.concatenate([cotangent[0], far_pack[block:]], axis=0).astype(jnp.float32)
    gain_in = gains[0:D]
    gain_attn = gains[D : 2 * D]
    gain_mlp = gains[2 * D : 3 * D]
    gain_out = gains[3 * D : 4 * D]
    gain_query = gains[4 * D : 4 * D + HD]
    gain_key = gains[4 * D + HD : 4 * D + 2 * HD]
    normed = rms_norm(tokens_f, gain_in)
    normed_b = normed.astype(jnp.bfloat16)
    q_raw = matmul(normed_b, w_q)
    k_raw = matmul(normed_b, full_k)
    v_raw = matmul(normed_b, full_v)

    def rotary(q_part, k_part, gq_part, gk_part):
        return queries_keys(q_part, k_part, gq_part, gk_part, places)

    (queries, keys_own), pull_rot = jax.vjp(rotary, q_raw, k_raw, gain_query, gain_key)
    heads = queries.shape[1]
    queries_b = queries.astype(jnp.bfloat16).reshape(2, block, heads, HD)
    kv_b = jnp.concatenate([keys_own, v_raw], axis=1).astype(jnp.bfloat16)
    kv_b = kv_b.reshape(2, block, 2 * HD)
    reach = WINDOW // block
    parts = [shifted(kv_b, "seq", distance) for distance in range(reach, 0, -1)]
    kv_all = jnp.concatenate(parts + [kv_b], axis=1)
    keys_all = kv_all[:, :, :HD]
    values_all = kv_all[:, :, HD:]
    span = (reach + 1) * block
    row_ids = jnp.arange(block, dtype=jnp.int32)[:, None]
    col_ids = jnp.arange(span, dtype=jnp.int32)[None, :]
    offsets = row_ids - col_ids + reach * block
    first_key = (lax.axis_index("seq") - reach) * block
    allowed = (
        (offsets >= 0)[None]
        & (offsets[None] <= jnp.minimum(places2[:, :, None], WINDOW - 1))
        & (first_key + col_ids >= 0)[None]
    )
    factor = HD ** (-0.5)
    raw_scores = (
        jnp.einsum("bthd,bkd->bhtk", queries_b, keys_all, preferred_element_type=jnp.float32)
        * factor
    )
    scores = jnp.where(allowed[:, None], raw_scores, NEGATIVE)
    exponent = jnp.exp(scores - jnp.max(scores, axis=-1, keepdims=True))
    probs_f = exponent / jnp.sum(exponent, axis=-1, keepdims=True)
    probs_b = probs_f.astype(jnp.bfloat16)
    attended = jnp.einsum(
        "bhtk,bkd->bthd", probs_b, values_all, preferred_element_type=jnp.float32
    )
    attended_b = attended.reshape(2 * block, heads * HD).astype(jnp.bfloat16)
    attn_raw = pair_sum(matmul(attended_b, w_o))
    attn_normed, pull_attn = jax.vjp(rms_norm, attn_raw, gain_attn)
    residual = tokens_f + attn_normed
    ffn_in, pull_mlp = jax.vjp(rms_norm, residual, gain_mlp)
    ffn_b = ffn_in.astype(jnp.bfloat16)
    gate_raw = matmul(ffn_b, w_gate)
    up_raw = matmul(ffn_b, w_up)
    hidden, pull_mix = jax.vjp(gelu_mix, gate_raw, up_raw)
    hidden_b = hidden.astype(jnp.bfloat16)
    down_raw = pair_sum(matmul(hidden_b, w_down))
    down_normed, pull_out = jax.vjp(rms_norm, down_raw, gain_out)
    output_b = (residual[:block] + down_normed[:block]).astype(jnp.bfloat16)
    d_down, d_gain_out = pull_out(d_out)
    d_down_b = d_down.astype(jnp.bfloat16)
    grad_down = inner_left(hidden_b, d_down_b)
    d_hidden = inner_right(d_down_b, w_down)
    d_gate, d_up = pull_mix(d_hidden)
    d_gate_b = d_gate.astype(jnp.bfloat16)
    d_up_b = d_up.astype(jnp.bfloat16)
    d_ffn = pair_sum(inner_right(d_gate_b, w_gate) + inner_right(d_up_b, w_up))
    grad_gate = inner_left(ffn_b, d_gate_b)
    grad_up = inner_left(ffn_b, d_up_b)
    d_from_mlp, d_gain_mlp = pull_mlp(d_ffn)
    d_residual = d_out + d_from_mlp
    d_attn, d_gain_attn = pull_attn(d_residual)
    d_attn_b = d_attn.astype(jnp.bfloat16)
    grad_o = inner_left(attended_b, d_attn_b)
    d_attended = inner_right(d_attn_b, w_o).astype(jnp.bfloat16).reshape(2, block, heads, HD)
    d_probs = jnp.einsum(
        "bthd,bkd->bhtk", d_attended, values_all, preferred_element_type=jnp.float32
    )
    row_total = jnp.sum(probs_f * d_probs, axis=-1, keepdims=True)
    d_scores = (probs_f * (d_probs - row_total)).astype(jnp.bfloat16)
    d_keys = (
        jnp.einsum("bhtk,bthd->bkd", d_scores, queries_b, preferred_element_type=jnp.float32)
        * factor
    )
    d_values = jnp.einsum(
        "bhtk,bthd->bkd", probs_b, d_attended, preferred_element_type=jnp.float32
    )
    d_kv = jnp.concatenate([d_keys, d_values], axis=2)
    d_kv_far = d_kv[:, : reach * block].astype(jnp.bfloat16)
    d_kv_own = d_kv[:, reach * block :]
    for distance in range(1, reach + 1):
        lower = (reach - distance) * block
        d_kv_own = d_kv_own + shifted(
            d_kv_far[:, lower : lower + block], "seq", -distance
        ).astype(jnp.float32)
    d_kv_own = pair_sum(d_kv_own).reshape(2 * block, 2 * HD)
    d_queries = (
        jnp.einsum("bhtk,bkd->bthd", d_scores, keys_all, preferred_element_type=jnp.float32)
        * factor
    ).reshape(2 * block, heads, HD)
    d_q_raw, d_k_raw, d_gain_query, d_gain_key = pull_rot((d_queries, d_kv_own[:, :HD]))
    d_q_b = d_q_raw.astype(jnp.bfloat16)
    d_kv_b = jnp.concatenate([d_k_raw, d_kv_own[:, HD:]], axis=1).astype(jnp.bfloat16)
    from_q = inner_right(d_q_b, w_q)
    far_q = swapped(from_q[block:].astype(jnp.bfloat16)).astype(jnp.float32)
    grad_q = inner_left(normed_b, d_q_b)
    d_k_half = lax.dynamic_slice_in_dim(d_kv_b[:, :HD], fsdp * half, half, 1)
    d_v_half = lax.dynamic_slice_in_dim(d_kv_b[:, HD:], fsdp * half, half, 1)
    grad_k = inner_left(normed_b, d_k_half)
    grad_v = inner_left(normed_b, d_v_half)
    d_normed = (
        from_q[:block]
        + far_q
        + inner_right(d_kv_b[:block, :HD], full_k)
        + inner_right(d_kv_b[:block, HD:], full_v)
    )
    d_from_in, d_gain_in = jax.vjp(rms_norm, tokens_f[:block], gain_in)[1](d_normed)
    d_tokens = d_residual[:block] + d_from_in
    grad_gains = jnp.concatenate(
        [
            d_gain_in,
            0.5 * d_gain_attn,
            0.5 * d_gain_mlp,
            0.5 * d_gain_out,
            d_gain_query,
            0.5 * d_gain_key,
        ]
    )
    columns = [grad_q, grad_k, grad_v, grad_gate, grad_up]
    if lax.axis_size("seq") == 16:
        reduced = reduce_planes(columns, [grad_down, grad_o], grad_gains, fsdp)
        flat_q, flat_k, flat_v, flat_gate, flat_up, flat_down, flat_o, flat_gains = reduced
    else:
        reduced = reduce_generic(columns, [grad_down, grad_o], fsdp)
        flat_q, flat_k, flat_v, flat_gate, flat_up, flat_down, flat_o = reduced
        flat_gains = lax.psum_scatter(
            grad_gains, ("seq", "fsdp"), scatter_dimension=0, tiled=True
        )
    return (
        output_b[None],
        d_tokens[None],
        flat_q,
        flat_k,
        flat_v,
        flat_o,
        flat_gate,
        flat_up,
        flat_down,
        flat_gains,
    )


def solution(mesh):
    in_specs = (
        P("fsdp", "seq", None),
        P(None, "fsdp"),
        P(None, "fsdp"),
        P(None, "fsdp"),
        P("fsdp", None),
        P(None, "fsdp"),
        P(None, "fsdp"),
        P("fsdp", None),
        P(),
        P("fsdp", "seq"),
        P("fsdp", "seq", None),
    )
    out_specs = (
        P("fsdp", "seq", None),
        P("fsdp", "seq", None),
        P(("seq", "fsdp")),
        P(("seq", "fsdp")),
        P(("seq", "fsdp")),
        P(("seq", "fsdp")),
        P(("seq", "fsdp")),
        P(("seq", "fsdp")),
        P(("seq", "fsdp")),
        P(("seq", "fsdp")),
    )
    return jax.shard_map(
        per_device, mesh=mesh, in_specs=in_specs, out_specs=out_specs, check_vma=False
    )
```
